256 devices in a mesh: seq: 128 (over y, z, x), head: 2 (over core).
Axes of the slice: x: 4, y: 4, z: 8, core: 2. Of those that a mesh axis runs over, the one named last changes fastest.
Arguments:
- mixer_input: bfloat16 [32768, 3584], P('seq', 'head'), may hold values from -6 to 6
- decay_rate: float32 [56, 32768], P('head', 'seq'), may hold values from 0 to 1
- state_in: bfloat16 [32768, 128], P('seq', 'head'), may hold values from -0.75 to 0.75
- state_out: bfloat16 [32768, 128], P('seq', 'head'), may hold values from -0.29882812 to 0.29882812
- skip_gain: float32 [56], P('head'), may hold values from 0.1 to 1.9
- att_queries: bfloat16 [32768, 3584], P('seq', 'head'), may hold values from -125 to 125
- att_keys: bfloat16 [32768, 3584], P('seq', 'head'), may hold values from -4.6 to 4.6
- att_values: bfloat16 [32768, 3584], P('seq', 'head'), may hold values from -60 to 60
- checkpoint_at: int32 [128], P('seq'), may hold values from 0 to 32767, as said below
- checkpoint_owner: int32 [128, 128], P('seq'), may hold values from 0 to 127, each once within a row
- block_owner: int32 [128, 128], P('seq'), may hold values from 0 to 127, each once within a row
Outputs:
- mixer_out: float32 [32768, 3584], P('seq', 'head')
- attention_out: bfloat16 [32768, 3584], P('seq', 'head')
- state_pool: float32 [128, 128, 1792], P('seq', None, 'head')
- cache_pool: bfloat16 [128, 256, 2, 3584], P('seq', None, None, 'head')
The draws below stay inside these ranges and needn't reach their ends.
Inputs may be any that keep to these rules, and one draw needn't show every extreme that they name: `checkpoint_at`: checkpoint b lies among positions b * 256 to (b + 1) * 256 - 1. `checkpoint_owner`: each row names every owner once. `block_owner`: each row names every owner once.
All inputs are finite; a program needn't handle non-finite values.
Results may differ from the reference program's by a relative error of at most 0.009.
Values may be sent and summed in bfloat16 or wider, within the bound.
No kernel may reach another device: no remote copies, remote signals or barrier semaphores. Data moves between devices by JAX's collectives and lax.ppermute only.
A program may use at most 320 MiB of HBM per device.

```python
import math
import jax
import jax.numpy as jnp
from jax import lax

MHEADS = 56
HDIM = 64
NSTATE = 64
NGROUPS = 2
AHEADS = 16
AHDIM = 224
TOK_DEV = 256
WIN = 2048
DOCUMENT_TOKENS = 32768
CHECKPOINTS = 128
OWNERS = 128
KVB = 2
POOLW = 1792
N_SEQ = 128
N_HEAD = 2


def shared_keys(key):
    return jnp.clip(jax.random.normal(key, (DOCUMENT_TOKENS, AHEADS * AHDIM), jnp.float32), -4.5, 4.5)


def draw_att_keys(key, part):
    shared = shared_keys(key)
    return shared.astype(jnp.bfloat16)


def draw_att_queries(key, part):
    key = jax.random.fold_in(key, 7)
    drawn = jnp.clip(jax.random.normal(key, (DOCUMENT_TOKENS, AHEADS * AHDIM), jnp.float32), -4.5, 4.5)
    return drawn.astype(jnp.bfloat16)


def draw_att_values(key, part):
    key = jax.random.fold_in(key, 11)
    block_count = DOCUMENT_TOKENS // TOK_DEV
    order = jax.random.permutation(jax.random.fold_in(key, 1), block_count)
    heavy_rank = jnp.argsort(order)
    block_scale = jnp.where(heavy_rank < 3, 10.0, 1.0).astype(jnp.float32)
    row_scale = jnp.repeat(block_scale, TOK_DEV)[:, None]
    base = jnp.clip(jax.random.normal(jax.random.fold_in(key, 2), (DOCUMENT_TOKENS, AHEADS * AHDIM), jnp.float32), -6.0, 6.0)
    return (base * row_scale).astype(jnp.bfloat16)


def draw_decay_rate(key, part):
    key = jax.random.fold_in(key, 3)
    chooser = jax.random.uniform(jax.random.fold_in(key, 1), (MHEADS,), jnp.float32)
    slow_rate = jnp.exp(jax.random.uniform(jax.random.fold_in(key, 2), (MHEADS,), jnp.float32, math.log(0.1), math.log(0.6))) / DOCUMENT_TOKENS
    fast_rate = jnp.exp(jax.random.uniform(jax.random.fold_in(key, 3), (MHEADS,), jnp.float32, math.log(1.0 / 60.0), math.log(1.0 / 20.0)))
    slow_share = 0.5
    per_head_rate = jnp.where(chooser < slow_share, slow_rate, fast_rate)
    block_count = DOCUMENT_TOKENS // TOK_DEV
    block_scale_factor = jnp.exp(jax.random.uniform(jax.random.fold_in(key, 4), (block_count,), jnp.float32, math.log(0.5), math.log(2.0)))
    block_scale_factor = jnp.repeat(block_scale_factor, TOK_DEV)
    jaggedness = jnp.exp(jax.random.uniform(jax.random.fold_in(key, 5), (MHEADS, DOCUMENT_TOKENS), jnp.float32, -0.7, 0.7))
    spike_position = jax.random.randint(jax.random.fold_in(key, 6), (3,), 0, DOCUMENT_TOKENS)
    spike_magnitude = jax.random.uniform(jax.random.fold_in(key, 7), (3,), jnp.float32, 0.22, 0.5)
    location_list = jnp.arange(DOCUMENT_TOKENS)
    spike_events = jnp.sum(jnp.where(location_list[None, :] == spike_position[:, None], spike_magnitude[:, None], 0.0), axis=0)
    decay_rates = per_head_rate[:, None] * block_scale_factor[None, :] * jaggedness + spike_events[None, :]
    return decay_rates.astype(jnp.float32)


def draw_checkpoint_at(key, part):
    key = jax.random.fold_in(key, 9)
    count = DOCUMENT_TOKENS // TOK_DEV
    jitter = jax.random.randint(key, (count,), 0, TOK_DEV)
    block_index = jnp.arange(count, dtype=jnp.int32)
    jitter = jnp.where(block_index == 0, 0, jitter)
    jitter = jnp.where(block_index == count - 1, TOK_DEV - 1, jitter)
    return (block_index * TOK_DEV + jitter).astype(jnp.int32)


def steps_of(stream_key, extent, cuts, low, high):
    def one(position, blocks):
        steps = jax.random.uniform(jax.random.fold_in(jax.random.fold_in(stream_key, 6), position), (blocks,), jnp.float32, low / len(cuts), high / len(cuts))
        return jnp.repeat(jnp.exp(steps), extent[position] // blocks).reshape((-1,) + (1,) * (len(extent) - position - 1))

    loudness = one(*cuts[0])
    for cut in cuts[1:]:
        loudness = loudness * one(*cut)
    return loudness


def bell_draw(stream_key, dims, deviation, reach, shards=(), held_as=jnp.bfloat16):
    array = deviation * jax.random.normal(stream_key, dims, jnp.float32)
    if shards:
        array = array * steps_of(stream_key, dims, shards, -0.22, 0.18)
    return jnp.clip(array, -reach, reach).astype(held_as)


def setup_inputs(seed: int = 0) -> dict:
    arg_keys = jax.random.split(jax.random.key(seed), 12)
    return {
        "mixer_input": bell_draw(arg_keys[0], (DOCUMENT_TOKENS, MHEADS * HDIM), 1.0, 6.0, ((0, 128), (1, 2))),
        "decay_rate": draw_decay_rate(jax.random.fold_in(arg_keys[11], 71), 0),
        "state_in": bell_draw(arg_keys[2], (DOCUMENT_TOKENS, NGROUPS * NSTATE), 0.125, 0.75, ((0, 128), (1, 2))),
        "state_out": bell_draw(arg_keys[3], (DOCUMENT_TOKENS, NGROUPS * NSTATE), 0.05, 0.29882812, ((0, 128), (1, 2))),
        "skip_gain": jnp.clip(1.0 + 0.18 * jax.random.normal(arg_keys[4], (MHEADS,), jnp.float32), 0.1, 1.9),
        "att_queries": draw_att_queries(jax.random.fold_in(arg_keys[11], 71), 0),
        "att_keys": draw_att_keys(jax.random.fold_in(arg_keys[11], 71), 0),
        "att_values": draw_att_values(jax.random.fold_in(arg_keys[11], 71), 0),
        "checkpoint_at": draw_checkpoint_at(jax.random.fold_in(arg_keys[11], 71), 0),
        "checkpoint_owner": jax.vmap(lambda own: jax.random.permutation(own, OWNERS))(jax.random.split(arg_keys[9], CHECKPOINTS)).reshape((CHECKPOINTS, OWNERS)).astype(jnp.int32),
        "block_owner": jax.vmap(lambda own: jax.random.permutation(own, OWNERS))(jax.random.split(arg_keys[10], CHECKPOINTS)).reshape((CHECKPOINTS, OWNERS)).astype(jnp.int32),
    }


def mixer_scan(mixer_input, decay_rate, state_in, state_out, skip_gain, checkpoint_at):
    per_group = MHEADS // NGROUPS

    def one_block(state, pieces):
        block_input, block_rate, block_write, block_read, spot = pieces
        tokens = block_input.shape[0]
        mix_heads = block_input.reshape(tokens, MHEADS, HDIM).astype(jnp.float32)
        write_groups = block_write.reshape(tokens, NGROUPS, NSTATE).astype(jnp.float32)
        read_groups = block_read.reshape(tokens, NGROUPS, NSTATE).astype(jnp.float32)
        write_heads = jnp.repeat(write_groups, per_group, axis=1)
        read_heads = jnp.repeat(read_groups, per_group, axis=1)
        log_decay = jnp.cumsum(-block_rate, axis=1)
        gram_groups = jnp.einsum("tgn,sgn->gts", read_groups, write_groups)
        gram_heads = jnp.repeat(gram_groups, per_group, axis=0)
        later_rows = jnp.arange(tokens)[:, None] >= jnp.arange(tokens)[None, :]
        spread = jnp.where(later_rows[None], log_decay[:, :, None] - log_decay[:, None, :], 0.0)
        decay_mat = jnp.where(later_rows[None], jnp.exp(spread), 0.0)
        mix_weights = (gram_heads * decay_mat).astype(jnp.bfloat16).astype(jnp.float32)
        inner_part = jnp.einsum("hts,shp->thp", mix_weights, mix_heads)
        carried = jnp.einsum("thn,hpn->thp", read_heads, state, precision=lax.Precision.HIGHEST)
        carried = carried * jnp.exp(log_decay).T[:, :, None]
        mixed = inner_part + carried + skip_gain[None, :, None] * mix_heads
        to_end = jnp.exp(log_decay[:, -1:] - log_decay)
        scaled_end = (mix_heads * to_end.T[:, :, None]).astype(jnp.bfloat16).astype(jnp.float32)
        local_end = jnp.einsum("thp,thn->hpn", scaled_end, write_heads)
        new_state = jnp.exp(log_decay[:, -1])[:, None, None] * state + local_end
        spot_log = lax.dynamic_slice_in_dim(log_decay, spot, 1, 1)
        before_spot = (jnp.arange(tokens, dtype=jnp.int32) <= spot)[None, :]
        to_spot = jnp.where(before_spot, jnp.exp(jnp.where(before_spot, spot_log - log_decay, 0.0)), 0.0)
        scaled_spot = (mix_heads * to_spot.T[:, :, None]).astype(jnp.bfloat16).astype(jnp.float32)
        spot_state = jnp.exp(spot_log)[:, :, None] * state + jnp.einsum("thp,thn->hpn", scaled_spot, write_heads)
        return new_state, (mixed.reshape(tokens, MHEADS * HDIM), spot_state)

    block_inputs = mixer_input.reshape(N_SEQ, TOK_DEV, MHEADS * HDIM)
    block_rates = decay_rate.reshape(MHEADS, N_SEQ, TOK_DEV).transpose(1, 0, 2)
    block_writes = state_in.reshape(N_SEQ, TOK_DEV, NGROUPS * NSTATE)
    block_reads = state_out.reshape(N_SEQ, TOK_DEV, NGROUPS * NSTATE)
    spots = (checkpoint_at - jnp.arange(N_SEQ, dtype=jnp.int32) * TOK_DEV).astype(jnp.int32)
    initial = jnp.zeros((MHEADS, HDIM, NSTATE), jnp.float32)
    final_state, outputs = lax.scan(one_block, initial, (block_inputs, block_rates, block_writes, block_reads, spots))
    return outputs[0].reshape(DOCUMENT_TOKENS, MHEADS * HDIM), outputs[1]


def windowed_attention(att_queries, att_keys, att_values):
    width = AHEADS * AHDIM
    padded_keys = jnp.concatenate([jnp.zeros((WIN, width), att_keys.dtype), att_keys], axis=0)
    padded_values = jnp.concatenate([jnp.zeros((WIN, width), att_values.dtype), att_values], axis=0)

    def one_block(block_index):
        first = (block_index * TOK_DEV).astype(jnp.int32)
        query_heads = lax.dynamic_slice_in_dim(att_queries, first, TOK_DEV, 0).reshape(TOK_DEV, AHEADS, AHDIM).astype(jnp.float32)
        key_heads = lax.dynamic_slice_in_dim(padded_keys, first, WIN + TOK_DEV, 0).reshape(WIN + TOK_DEV, AHEADS, AHDIM).astype(jnp.float32)
        value_heads = lax.dynamic_slice_in_dim(padded_values, first, WIN + TOK_DEV, 0).reshape(WIN + TOK_DEV, AHEADS, AHDIM).astype(jnp.float32)
        scores = jnp.einsum("thd,shd->hts", query_heads, key_heads) * (AHDIM ** -0.5)
        query_place = first + jnp.arange(TOK_DEV, dtype=jnp.int32)
        key_place = first - WIN + jnp.arange(WIN + TOK_DEV, dtype=jnp.int32)
        distance = query_place[:, None] - key_place[None, :]
        allowed = ((distance >= 0) & (distance < WIN) & (key_place[None, :] >= 0))[None]
        masked = jnp.where(allowed, scores, -1e30)
        largest = jnp.max(masked, axis=2)
        weights = jnp.where(allowed, jnp.exp(masked - largest[:, :, None]), 0.0)
        denom = jnp.sum(weights, axis=2)
        rounded = weights.astype(jnp.bfloat16).astype(jnp.float32)
        numer = jnp.einsum("hts,shd->thd", rounded, value_heads)
        return (numer / denom.T[:, :, None]).astype(jnp.bfloat16).reshape(TOK_DEV, width)

    blocks = lax.map(one_block, jnp.arange(N_SEQ, dtype=jnp.int32))
    return blocks.reshape(DOCUMENT_TOKENS, width)


def owner_order(owner_table):
    slots = jnp.arange(OWNERS, dtype=jnp.int32)
    return jnp.argmax(owner_table[:, None, :] == slots[None, :, None], axis=2).astype(jnp.int32)


def reference(mixer_input, decay_rate, state_in, state_out, skip_gain, att_queries, att_keys, att_values, checkpoint_at, checkpoint_owner, block_owner):
    mixer_out, spot_states = mixer_scan(mixer_input, decay_rate, state_in, state_out, skip_gain, checkpoint_at)
    attention_out = windowed_attention(att_queries, att_keys, att_values)
    row_index = jnp.arange(N_SEQ, dtype=jnp.int32)[:, None]
    state_pieces = spot_states.reshape(N_SEQ, N_HEAD, OWNERS, -1)
    state_order = owner_order(checkpoint_owner)
    picked_states = state_pieces[row_index, :, state_order]
    state_pool = picked_states.transpose(1, 0, 2, 3).reshape(OWNERS, CHECKPOINTS, POOLW)
    width = AHEADS * AHDIM
    key_blocks = att_keys.reshape(N_SEQ, OWNERS, KVB, width)
    value_blocks = att_values.reshape(N_SEQ, OWNERS, KVB, width)
    paired = jnp.stack([key_blocks, value_blocks], axis=3)
    block_order = owner_order(block_owner)
    picked_blocks = paired[row_index, block_order]
    cache_pool = picked_blocks.transpose(1, 0, 2, 3, 4).reshape(OWNERS, N_SEQ * KVB, 2, width)
    return mixer_out, attention_out, state_pool, cache_pool
```

```python
import functools

import jax
import jax.numpy as jnp
from jax import lax
from jax.experimental import pallas as pl
from jax.experimental.pallas import tpu as pltpu
from jax.sharding import PartitionSpec as P

HDIM = 64
NSTATE = 64
AHDIM = 224
TOK = 256
ROW = 4
PACK = AHDIM + 16
SCALE = AHDIM**-0.5 * 1.4426950408889634
LOWEST = -1e30
HEAVY = 4 * 10**10
BF = jnp.bfloat16
F32 = jnp.float32
HIGHEST = lax.Precision.HIGHEST


def call(kernel, out_shape, in_smem, *args, name, scratch=(), after=(), mib=16, flops=0):
    specs = [
        pl.BlockSpec(memory_space=pltpu.SMEM if i in in_smem else pltpu.VMEM)
        for i in range(len(args))
    ] + [pl.BlockSpec(memory_space=pl.ANY)] * len(after)

    def run(*refs):
        kernel(*refs[: len(args)], *refs[len(args) + len(after) :])

    outs = jax.tree.map(lambda _: pl.BlockSpec(memory_space=pltpu.VMEM), out_shape)
    return pl.pallas_call(
        run,
        out_shape=out_shape,
        in_specs=specs,
        out_specs=outs,
        scratch_shapes=list(scratch),
        compiler_params=pltpu.CompilerParams(vmem_limit_bytes=mib * 2**20),
        cost_estimate=pl.CostEstimate(flops=flops, bytes_accessed=0, transcendentals=0),
        name=name,
    )(*args, *after)


def shape(*dims, dtype=BF):
    return jax.ShapeDtypeStruct(dims, dtype)


def turn(x_ref, turned):
    for start in range(0, x_ref.shape[1], 128):
        turned[start : start + 128, :] = x_ref[:, start : start + 128].T


def pair_rows(turned, pair, odd):
    at = pair * (2 * AHDIM) + odd * AHDIM
    return turned[pl.ds(pl.multiple_of(at, 32), AHDIM), :]


def prep_kernel(place_ref, q_ref, k_ref, v_ref, *refs):
    outputs, (q, k, v) = refs[:ROW], refs[ROW:]
    for x_ref, turned in ((k_ref, k), (v_ref, v), (q_ref, q)):
        turn(x_ref, turned)
    for d in range(ROW):
        pair = lax.rem(place_ref[0] + d, ROW)
        for i, (turned, odd) in enumerate(((k, 0), (v, 0), (q, 1), (q, 0), (k, 1), (v, 1))):
            outputs[d][i * AHDIM : (i + 1) * AHDIM, :] = pair_rows(turned, pair, odd)


def gather_kernel(place_ref, *refs):
    kv_ref, q_ref, second_ref = refs[ROW:]
    for d in range(ROW):
        block = lax.rem(place_ref[0] + ROW - d, ROW)
        kv_ref[block] = refs[d][0 : 2 * AHDIM, :]
        q_ref[block] = refs[d][2 * AHDIM : 3 * AHDIM, :]
        second_ref[block] = refs[d][3 * AHDIM : 6 * AHDIM, :]


def absorb(q, keys, values, mode, qb, state):
    if mode == "causal":
        blocks = range(0, qb + 1)
    elif mode == "tail":
        blocks = range(qb, ROW)
    else:
        blocks = range(ROW)
    scores = []
    for kb in blocks:
        s = lax.dot_general(keys(kb), q, (((0,), (0,)), ((), ())), preferred_element_type=F32)
        if kb == qb and mode != "full":
            s_at = lax.broadcasted_iota(jnp.int32, s.shape, 0)
            t_at = lax.broadcasted_iota(jnp.int32, s.shape, 1)
            s = jnp.where(s_at <= t_at if mode == "causal" else s_at > t_at, s, LOWEST)
        scores.append(s)
    best = functools.reduce(jnp.maximum, [jnp.max(s, axis=0, keepdims=True) for s in scores])
    if state is not None:
        best = jnp.maximum(best, state[0])
    total, product = 0.0, 0.0
    for kb, s in zip(blocks, scores):
        p = jnp.exp2((s - best) * SCALE)
        if kb == qb and mode == "tail":
            s_at = lax.broadcasted_iota(jnp.int32, s.shape, 0)
            t_at = lax.broadcasted_iota(jnp.int32, s.shape, 1)
            p = jnp.where(s_at > t_at, p, 0.0)
        total = total + jnp.sum(p, axis=0, keepdims=True)
        product = product + jnp.dot(values(kb), p.astype(BF), preferred_element_type=F32)
    if state is not None:
        shrink = jnp.exp2((state[0] - best) * SCALE)
        total = total + state[1] * shrink
        product = product + state[2] * shrink
    return best, total, product


def rows_of(ref, first):
    return lambda kb: ref[kb, first : first + AHDIM, :]


def store_state(state, stat_ref, acc_ref, qb):
    stat_ref[qb, 0:1, :] = state[0]
    stat_ref[qb, 1:2, :] = state[1]
    acc_ref[qb] = state[2]


def load_state(stat_ref, acc_ref, qb):
    return stat_ref[qb, 0:1, :], stat_ref[qb, 1:2, :], acc_ref[qb]


def parts_of(x):
    high = x.astype(BF).astype(F32)
    rest = x - high
    middle = rest.astype(BF).astype(F32)
    return high, middle, (rest - middle).astype(BF).astype(F32)


def store_packed(state, ref, qb):
    best, total, product = state
    ref[qb, 0:AHDIM, :] = (product / jnp.where(total > 0.0, total, 1.0)).astype(BF)
    row = lax.broadcasted_iota(jnp.int32, (16, TOK), 0)
    stats = jnp.zeros((16, TOK), F32)
    for i, part in enumerate(parts_of(best) + parts_of(total)):
        stats = jnp.where(row == i, part, stats)
    ref[qb, AHDIM:PACK, :] = stats.astype(BF)


def merge_packed(state, ref, qb):
    stats = ref[qb, AHDIM:PACK, :].astype(F32)
    best = stats[0:1] + stats[1:2] + stats[2:3]
    total = stats[3:4] + stats[4:5] + stats[5:6]
    best = jnp.where(total > 0.0, best, LOWEST)
    top = jnp.maximum(best, state[0])
    other = jnp.exp2((best - top) * SCALE) * total
    mine = jnp.exp2((state[0] - top) * SCALE)
    product = state[2] * mine + ref[qb, 0:AHDIM, :].astype(F32) * other
    return top, state[1] * mine + other, product


def own_kernel(kv_ref, q_ref, second_ref, a_stat, a_acc, b_stat, b_acc):
    for qb in range(ROW):
        state = absorb(
            second_ref[qb, 0:AHDIM, :],
            rows_of(kv_ref, 0),
            rows_of(kv_ref, AHDIM),
            "causal",
            qb,
            None,
        )
        store_state(state, a_stat, a_acc, qb)
        state = absorb(
            q_ref[qb],
            rows_of(second_ref, AHDIM),
            rows_of(second_ref, 2 * AHDIM),
            "causal",
            qb,
            None,
        )
        store_state(state, b_stat, b_acc, qb)


def nearer_kernel(row_ref, second_ref, kv_ref, stat_in, acc_in, stat_ref, acc_ref):
    stat_ref[...] = stat_in[...]
    acc_ref[...] = acc_in[...]

    @pl.when(row_ref[0] >= 1)
    def _():
        for qb in range(ROW):
            state = absorb(
                second_ref[qb, 0:AHDIM, :],
                rows_of(kv_ref, 0),
                rows_of(kv_ref, AHDIM),
                "full",
                qb,
                load_state(stat_in, acc_in, qb),
            )
            store_state(state, stat_ref, acc_ref, qb)


def next_kernel(q_ref, second_ref, stat_ref, acc_ref):
    for qb in range(ROW):
        state = absorb(
            q_ref[qb],
            rows_of(second_ref, AHDIM),
            rows_of(second_ref, 2 * AHDIM),
            "full",
            qb,
            None,
        )
        store_state(state, stat_ref, acc_ref, qb)


def after_kernel(q_ref, second_ref, packed_ref):
    for qb in range(ROW):
        state = absorb(
            q_ref[qb],
            rows_of(second_ref, AHDIM),
            rows_of(second_ref, 2 * AHDIM),
            "tail",
            qb,
            None,
        )
        store_packed(state, packed_ref, qb)


def join_kernel(stat_in, acc_in, packed_in, packed_ref):
    for qb in range(ROW):
        store_packed(merge_packed(load_state(stat_in, acc_in, qb), packed_in, qb), packed_ref, qb)


def last_kernel(
    row_ref, place_ref, second_ref, kv_ref, a_stat, a_acc, b_stat, b_acc, packed_in, *refs
):
    out_ref = refs[ROW]
    for qb in range(ROW):
        _, total, product = merge_packed(load_state(b_stat, b_acc, qb), packed_in, qb)
        out_ref[qb, AHDIM : 2 * AHDIM, :] = (product / total).astype(BF)
        _, total, product = load_state(a_stat, a_acc, qb)
        out_ref[qb, 0:AHDIM, :] = (product / total).astype(BF)

    @pl.when(row_ref[0] >= 2)
    def _():
        for qb in range(ROW):
            _, total, product = absorb(
                second_ref[qb, 0:AHDIM, :],
                rows_of(kv_ref, 0),
                rows_of(kv_ref, AHDIM),
                "tail",
                qb,
                load_state(a_stat, a_acc, qb),
            )
            out_ref[qb, 0:AHDIM, :] = (product / total).astype(BF)

    for d in range(ROW):
        refs[d][...] = out_ref[lax.rem(place_ref[0] + d, ROW)]


def back_kernel(place_ref, *refs):
    out_ref, turned = refs[ROW:]
    for d in range(ROW):
        pair = lax.rem(place_ref[0] + ROW - d, ROW)
        at = pl.multiple_of(pair * (2 * AHDIM), 32)
        turned[pl.ds(at, 2 * AHDIM), :] = refs[d][...]
    for start in range(0, turned.shape[0], 128):
        out_ref[:, start : start + 128] = turned[start : start + 128, :].T


def blocks_kernel(owner_ref, k_ref, v_ref, state_ref, send_ref, slots):
    owners = owner_ref.shape[1]
    pieces = k_ref.shape[1] // 128
    rows = 4 * pieces + 8
    owner = lax.broadcasted_iota(jnp.int32, (owners, owners), 0)
    pick = (owner_ref[...] == owner).astype(BF)
    block = lax.broadcasted_iota(jnp.int32, (owners, 2 * owners), 0)
    at = lax.broadcasted_iota(jnp.int32, (owners, 2 * owners), 1)
    for i in range(2):
        places = jnp.dot(pick, (at == 2 * block + i).astype(BF), preferred_element_type=F32)
        places = places.astype(BF)
        for kind, ref in enumerate((k_ref, v_ref)):
            picked = jnp.dot(places, ref[...], preferred_element_type=F32)
            for j in range(pieces):
                slots[pl.ds((i * pieces + j) * 2 + kind, owners, stride=rows), :] = picked[
                    :, j * 128 : (j + 1) * 128
                ]
    for device in range(owners):
        slots[device * rows + 4 * pieces : (device + 1) * rows, :] = state_ref[
            device * 8 : (device + 1) * 8, :
        ]
    send_ref[...] = slots[...].astype(BF)


def expand(x, heads):
    head = lax.broadcasted_iota(jnp.int32, (heads, heads * HDIM), 0)
    column = lax.broadcasted_iota(jnp.int32, (heads, heads * HDIM), 1)
    hot = (column // HDIM == head).astype(F32)
    return jnp.dot(x, hot, precision=HIGHEST, preferred_element_type=F32)


def state_kernel(x_ref, rate_ref, write_ref, cum_ref, turned_ref, slots):
    heads = rate_ref.shape[0]
    half = heads // 2 * HDIM
    rate = rate_ref[...]
    first = lax.broadcasted_iota(jnp.int32, (TOK, TOK), 0)
    second = lax.broadcasted_iota(jnp.int32, (TOK, TOK), 1)
    cum_ref[...] = -jnp.dot(
        rate, (first <= second).astype(F32), precision=HIGHEST, preferred_element_type=F32
    )
    turned = -lax.dot_general(
        (second <= first).astype(F32),
        rate,
        (((1,), (1,)), ((), ())),
        precision=HIGHEST,
        preferred_element_type=F32,
    )
    turned_ref[...] = turned
    end = turned[TOK - 1 : TOK, :]
    scaled = (x_ref[...].astype(F32) * expand(jnp.exp(end - turned), heads)).astype(BF)
    local = lax.dot_general(
        write_ref[...], scaled, (((0,), (0,)), ((), ())), preferred_element_type=F32
    )
    for side in range(2):
        for k in range(half // 128):
            start = side * half + k * 128
            slots[pl.ds(side * NSTATE * 8 + k, NSTATE, stride=8), :] = local[:, start : start + 128]
    lane = lax.broadcasted_iota(jnp.int32, (heads, 128), 1)
    head = lax.broadcasted_iota(jnp.int32, (heads, 128), 0)
    for side in range(2):
        tail = jnp.zeros((1, 128), F32)
        for i, part in enumerate(parts_of(end)):
            hot = (lane == 3 * (head - side * (heads // 2)) + i) & (head // (heads // 2) == side)
            tail = tail + jnp.dot(
                part, hot.astype(F32), precision=HIGHEST, preferred_element_type=F32
            )
        slots[pl.ds(side * NSTATE * 8 + half // 128, NSTATE, stride=8), :] = jnp.broadcast_to(
            tail, (NSTATE, 128)
        )


def scan_kernel(got_ref, out_ref, state, decay):
    blocks = state.shape[0] // 8
    rows = got_ref.shape[0] // blocks
    for b in range(blocks):
        state[b * 8 : (b + 1) * 8, :] = got_ref[(b + 1) * rows - 16 : (b + 1) * rows, :].astype(
            F32
        )[8:16]
    tail = state[pl.ds(7, blocks, stride=8), :].astype(BF)
    part = lax.broadcasted_iota(jnp.int32, (128, 128), 0)
    column = lax.broadcasted_iota(jnp.int32, (128, 128), 1)
    for k in range(7):
        hot = (part // 3 == 2 * k + column // HDIM).astype(BF)
        decay[pl.ds(k, blocks, stride=8), :] = jnp.exp(
            jnp.dot(tail, hot, preferred_element_type=F32)
        )
    decay[pl.ds(7, blocks, stride=8), :] = jnp.zeros((blocks, 128), F32)

    def step(b, carry):
        at = pl.ds(pl.multiple_of(b * 8, 8), 8)
        after = decay[at, :] * carry + state[at, :]
        state[at, :] = carry
        return after

    lax.fori_loop(0, blocks, step, jnp.zeros((8, 128), F32), unroll=8)
    out_ref[...] = state[...].astype(BF)


def cache_kernel(got_ref, out_ref, slots):
    blocks = out_ref.shape[0]
    pieces = out_ref.shape[3] // 128
    rows = 4 * pieces + 8
    for k in range(blocks // 8):
        slots[k * 8 : (k + 1) * 8] = (
            got_ref[k * 8 * rows : (k + 1) * 8 * rows, :].astype(F32).reshape(8, rows, 128)
        )
    for i in range(2):
        for j in range(pieces):
            at = (i * pieces + j) * 2
            out_ref[:, i, :, j * 128 : (j + 1) * 128] = slots[:, at : at + 2, :].astype(BF)


def inner_kernel(
    spot_ref, x_ref, cum_ref, turned_ref, write_ref, read_ref, gain_ref, out_ref, spot_ref_out
):
    heads = cum_ref.shape[0]
    write = write_ref[...]
    turned = turned_ref[...]
    gram = lax.dot_general(
        read_ref[...], write, (((1,), (1,)), ((), ())), preferred_element_type=F32
    )
    t_at = lax.broadcasted_iota(jnp.int32, (TOK, TOK), 0)
    s_at = lax.broadcasted_iota(jnp.int32, (TOK, TOK), 1)
    later = t_at >= s_at
    left = lax.broadcasted_iota(jnp.int32, (TOK, 2 * HDIM), 1) < HDIM
    gain = expand(gain_ref[...], heads)
    for pair in range(heads // 2):
        columns = slice(pair * 2 * HDIM, (pair + 1) * 2 * HDIM)
        x = x_ref[:, columns]
        inner = []
        for h in (2 * pair, 2 * pair + 1):
            spread = jnp.where(later, turned[:, h : h + 1] - cum_ref[h : h + 1, :], LOWEST)
            weights = (gram * jnp.exp(spread)).astype(BF)
            inner.append(jnp.dot(weights, x, preferred_element_type=F32))
        out_ref[:, columns] = jnp.where(left, inner[0], inner[1]) + gain[:, columns] * x.astype(
            F32
        )
    spot = spot_ref[0]
    position = lax.broadcasted_iota(jnp.int32, (TOK, heads), 0)
    to_spot = jnp.exp(jnp.where(position <= spot, spot_log(turned, spot) - turned, LOWEST))
    scaled = (x_ref[...].astype(F32) * expand(to_spot, heads)).astype(BF)
    spot_ref_out[...] = lax.dot_general(
        write, scaled, (((0,), (0,)), ((), ())), preferred_element_type=F32
    )


def spot_log(turned, spot):
    position = lax.broadcasted_iota(jnp.int32, turned.shape, 0)
    return jnp.sum(jnp.where(position == spot, turned, 0.0), axis=0, keepdims=True)


def mixer_kernel(
    spot_ref,
    owner_ref,
    turned_ref,
    read_ref,
    inner_ref,
    local_ref,
    came_ref,
    out_ref,
    send_ref,
    slots,
    rows,
    flat,
):
    heads = turned_ref.shape[1]
    half = heads // 2 * HDIM
    turned = turned_ref[...]
    slots[...] = came_ref[...].astype(F32)
    arriving = jnp.concatenate(
        [
            slots[pl.ds(side * NSTATE * 8 + k, NSTATE, stride=8), :]
            for side in range(2)
            for k in range(half // 128)
        ],
        axis=1,
    )
    carried = jnp.dot(read_ref[...], arriving.astype(BF), preferred_element_type=F32)
    out_ref[...] = inner_ref[...] + carried * expand(jnp.exp(turned), heads)
    at_spot = expand(jnp.exp(spot_log(turned, spot_ref[0])), heads)
    state = arriving * at_spot + local_ref[...]
    rows[:, 0:NSTATE] = state.T
    even = rows[pl.ds(0, heads * HDIM // 2, stride=2), :]
    odd = pltpu.roll(rows[pl.ds(1, heads * HDIM // 2, stride=2), :], NSTATE, 1)
    lane = lax.broadcasted_iota(jnp.int32, even.shape, 1)
    flat[0 : heads * HDIM // 2, :] = jnp.where(lane < NSTATE, even, odd)
    for piece in range(owner_ref.shape[1]):
        at = pl.multiple_of(owner_ref[0, piece] * 8, 8)
        slots[pl.ds(at, 8), :] = flat[7 * piece : 7 * piece + 8, :]
    send_ref[...] = slots[...].astype(BF)


def pool_kernel(got_ref, out_ref, slots):
    slots[...] = got_ref[...].astype(F32)
    blocks = out_ref.shape[1]
    for k in range(7):
        out_ref[0, :, k * 128 : (k + 1) * 128] = slots[pl.ds(k, blocks, stride=8), :]


def to_all(x):
    return lax.all_to_all(x, "seq", split_axis=0, concat_axis=0, tiled=True)


def in_row(parts):
    count = lax.axis_size("seq")
    return [parts[0]] + [
        lax.ppermute(
            parts[d],
            "seq",
            [(i, i // ROW * ROW + (i + d) % ROW) for i in range(count)],
        )
        for d in range(1, ROW)
    ]


def shift(x, distance):
    devices = range(lax.axis_size("seq"))
    return lax.ppermute(x, "seq", [(i - distance, i) for i in devices if i - distance in devices])


def body(
    mixer_input,
    decay_rate,
    state_in,
    state_out,
    skip_gain,
    att_queries,
    att_keys,
    att_values,
    checkpoint_at,
    checkpoint_owner,
    block_owner,
):
    position = lax.axis_index("seq")
    owners = lax.axis_size("seq")
    tokens, width = mixer_input.shape
    heads = decay_rate.shape[0]
    row = (position // ROW).astype(jnp.int32)[None]

    place = (position % ROW).astype(jnp.int32)[None]
    parts = call(
        prep_kernel,
        (shape(6 * AHDIM, TOK),) * ROW,
        (0,),
        place,
        att_queries,
        att_keys,
        att_values,
        name="prep",
        scratch=[pltpu.VMEM((width, TOK), BF)] * 3,
    )
    parts = in_row(parts)

    block_len = tokens // owners
    lanes = width // 128
    cum, turned, state_send = call(
        state_kernel,
        (
            shape(heads, TOK, dtype=F32),
            shape(TOK, heads, dtype=F32),
            shape(owners * 8, 128, dtype=F32),
        ),
        (),
        mixer_input,
        decay_rate,
        state_in,
        name="state",
    )
    send = call(
        blocks_kernel,
        shape(owners * (4 * lanes + 8), 128),
        (),
        block_owner,
        att_keys,
        att_values,
        state_send,
        name="blocks",
        scratch=[pltpu.VMEM((owners * (4 * lanes + 8), 128), F32)],
        mib=24,
    )
    spot = (checkpoint_at - position * tokens).astype(jnp.int32)
    inner, spot_local = call(
        inner_kernel,
        (shape(tokens, width, dtype=F32), shape(NSTATE, width, dtype=F32)),
        (0,),
        spot,
        mixer_input,
        cum,
        turned,
        state_in,
        state_out,
        skip_gain[None, :],
        name="inner",
        after=(send,),
    )
    got = to_all(send.reshape(owners, 4 * lanes + 8, 128))
    kv_own, q_own, second = call(
        gather_kernel,
        (shape(ROW, 2 * AHDIM, TOK), shape(ROW, AHDIM, TOK), shape(ROW, 3 * AHDIM, TOK)),
        (0,),
        place,
        *parts,
        name="gather",
        after=(inner,),
    )
    kv_near = shift(kv_own, ROW)
    q_next = shift(q_own, -ROW)
    stat, acc = shape(ROW, 8, TOK, dtype=F32), shape(ROW, AHDIM, TOK, dtype=F32)
    packed = shape(ROW, PACK, TOK)
    kv_far = shift(kv_near, ROW)
    q_after = shift(q_next, -ROW)
    a_stat, a_acc, b_stat, b_acc = call(
        own_kernel, (stat, acc, stat, acc), (), kv_own, q_own, second, name="own", flops=HEAVY
    )
    n_stat, n_acc = call(
        next_kernel, (stat, acc), (), q_next, second, name="next", flops=HEAVY, after=(a_stat,)
    )
    entering = call(
        scan_kernel,
        shape(owners * 8, 128),
        (),
        got.reshape(-1, 128),
        name="scan",
        after=(n_stat,),
        scratch=[pltpu.VMEM((owners * 8, 128), F32)] * 2,
    )
    came = to_all(entering.reshape(owners, 8, 128)).reshape(owners * 8, 128)
    after = call(after_kernel, packed, (), q_after, second, name="after", flops=HEAVY, after=(n_stat,))
    after = shift(after, ROW)
    a_stat, a_acc = call(
        nearer_kernel, (stat, acc), (0,), row, second, kv_near, a_stat, a_acc, name="nearer", flops=HEAVY
    )
    join_send = call(join_kernel, packed, (), n_stat, n_acc, after, name="join", flops=HEAVY, after=(a_stat,))
    joined = shift(join_send, ROW)
    out = call(
        last_kernel,
        (shape(2 * AHDIM, TOK),) * ROW,
        (0, 1),
        row,
        place,
        second,
        kv_far,
        a_stat,
        a_acc,
        b_stat,
        b_acc,
        joined,
        name="last", flops=HEAVY,
        scratch=[pltpu.VMEM((ROW, 2 * AHDIM, TOK), BF)],
    )
    attention_out = call(
        back_kernel,
        shape(TOK, width),
        (0,),
        place,
        *in_row(out),
        name="back",
        scratch=[pltpu.VMEM((width, TOK), BF)],
    )

    mixer_out, pool_send = call(
        mixer_kernel,
        (shape(tokens, width, dtype=F32), shape(owners * 8, 128)),
        (0, 1),
        spot,
        checkpoint_owner,
        turned,
        state_out,
        inner,
        spot_local,
        came,
        name="mixer",
        after=(a_stat,),
        scratch=[
            pltpu.VMEM((owners * 8, 128), F32),
            pltpu.VMEM((width, 2 * NSTATE), F32),
            pltpu.VMEM((width // 2 + 8, 128), F32),
        ],
    )
    cache_pool = call(
        cache_kernel,
        shape(owners, block_len, 2, width),
        (),
        got.reshape(-1, 128),
        name="cache",
        scratch=[pltpu.VMEM((owners, 4 * lanes + 8, 128), F32)],
        mib=24,
        after=(pool_send,),
    ).reshape(1, owners * block_len, 2, width)
    pool_got = to_all(pool_send.reshape(owners, 8, 128)).reshape(owners * 8, 128)
    state_pool = call(
        pool_kernel,
        shape(1, owners, width // 2, dtype=F32),
        (),
        pool_got,
        name="pool",
        scratch=[pltpu.VMEM((owners * 8, 128), F32)],
    )
    return (mixer_out, attention_out, state_pool, cache_pool)


def solution(mesh):
    placed = (
        P("seq", "head"),
        P("head", "seq"),
        P("seq", "head"),
        P("seq", "head"),
        P("head"),
        P("seq", "head"),
        P("seq", "head"),
        P("seq", "head"),
        P("seq"),
        P("seq", None),
        P("seq", None),
    )
    return jax.shard_map(
        body,
        mesh=mesh,
        in_specs=placed,
        out_specs=(
            P("seq", "head"),
            P("seq", "head"),
            P("seq", None, "head"),
            P("seq", None, None, "head"),
        ),
        check_vma=False,
    )
```

```python
import functools

import jax
import jax.numpy as jnp
from jax import lax
from jax.experimental import pallas as pl
from jax.experimental.pallas import tpu as pltpu
from jax.sharding import PartitionSpec as P

HDIM = 64
NSTATE = 64
AHDIM = 224
TOK = 256
ROW = 4
PACK = AHDIM + 16
SCALE = AHDIM**-0.5 * 1.4426950408889634
LOWEST = -1e30
HEAVY = 4 * 10**10
FIRST = 6
BF = jnp.bfloat16
F32 = jnp.float32
HIGHEST = lax.Precision.HIGHEST


def call(kernel, out_shape, in_smem, *args, name, scratch=(), after=(), mib=16, flops=0):
    specs = [
        pl.BlockSpec(memory_space=pltpu.SMEM if i in in_smem else pltpu.VMEM)
        for i in range(len(args))
    ] + [pl.BlockSpec(memory_space=pl.ANY)] * len(after)

    many = isinstance(out_shape, tuple)
    out_shapes = (out_shape if many else (out_shape,)) + (shape(8, 128, dtype=F32),)
    first_out = len(args) + len(after)
    token = first_out + len(out_shapes) - 1

    def run(*refs):
        kernel(*refs[: len(args)], *refs[first_out:token], *refs[token + 1 :])
        refs[token][...] = jnp.zeros((8, 128), F32)

    results = pl.pallas_call(
        run,
        out_shape=out_shapes,
        in_specs=specs,
        out_specs=tuple(pl.BlockSpec(memory_space=pltpu.VMEM) for _ in out_shapes),
        scratch_shapes=list(scratch),
        compiler_params=pltpu.CompilerParams(vmem_limit_bytes=mib * 2**20),
        cost_estimate=pl.CostEstimate(flops=flops, bytes_accessed=0, transcendentals=0),
        name=name,
    )(*args, *after)
    return (results[:-1] if many else results[0]), results[-1]


def shape(*dims, dtype=BF):
    return jax.ShapeDtypeStruct(dims, dtype)


def turn(x_ref, turned):
    for start in range(0, x_ref.shape[1], 128):
        turned[start : start + 128, :] = x_ref[:, start : start + 128].T


def pair_rows(turned, pair, odd):
    at = pair * (2 * AHDIM) + odd * AHDIM
    return turned[pl.ds(pl.multiple_of(at, 32), AHDIM), :]


def prep_kernel(place_ref, q_ref, k_ref, v_ref, *refs):
    outputs, (q, k, v) = refs[:ROW], refs[ROW:]
    for x_ref, turned in ((k_ref, k), (v_ref, v), (q_ref, q)):
        turn(x_ref, turned)
    for d in range(ROW):
        pair = lax.rem(place_ref[0] + d, ROW)
        for i, (turned, odd) in enumerate(((k, 0), (v, 0), (q, 1), (q, 0), (k, 1), (v, 1))):
            outputs[d][i * AHDIM : (i + 1) * AHDIM, :] = pair_rows(turned, pair, odd)


def gather_kernel(place_ref, *refs):
    kv_ref, q_ref, second_ref = refs[ROW:]
    for d in range(ROW):
        block = lax.rem(place_ref[0] + ROW - d, ROW)
        kv_ref[block] = refs[d][0 : 2 * AHDIM, :]
        q_ref[block] = refs[d][2 * AHDIM : 3 * AHDIM, :]
        second_ref[block] = refs[d][3 * AHDIM : 6 * AHDIM, :]


def absorb(q, keys, values, mode, qb, state):
    if mode == "causal":
        blocks = range(0, qb + 1)
    elif mode == "tail":
        blocks = range(qb, ROW)
    else:
        blocks = range(ROW)
    scores = []
    for kb in blocks:
        s = jnp.dot(keys(kb), q, preferred_element_type=F32)
        if kb == qb and mode != "full":
            s_at = lax.broadcasted_iota(jnp.int32, s.shape, 0)
            t_at = lax.broadcasted_iota(jnp.int32, s.shape, 1)
            s = jnp.where(s_at <= t_at if mode == "causal" else s_at > t_at, s, LOWEST)
        scores.append(s)
    best = functools.reduce(jnp.maximum, [jnp.max(s, axis=0, keepdims=True) for s in scores])
    if state is not None:
        best = jnp.maximum(best, state[0])
    total, product = 0.0, 0.0
    for kb, s in zip(blocks, scores):
        p = jnp.exp2((s - best) * SCALE)
        if kb == qb and mode == "tail":
            s_at = lax.broadcasted_iota(jnp.int32, s.shape, 0)
            t_at = lax.broadcasted_iota(jnp.int32, s.shape, 1)
            p = jnp.where(s_at > t_at, p, 0.0)
        total = total + jnp.sum(p, axis=0, keepdims=True)
        product = product + jnp.dot(values(kb), p.astype(BF), preferred_element_type=F32)
    if state is not None:
        shrink = jnp.exp2((state[0] - best) * SCALE)
        total = total + state[1] * shrink
        product = product + state[2] * shrink
    return best, total, product


def rows_of(ref, first):
    return lambda kb: ref[kb, first : first + AHDIM, :]


def keys_of(ref, first):
    turned = [ref[kb, first : first + AHDIM, :].T for kb in range(ROW)]
    return lambda kb: turned[kb]


def store_state(state, stat_ref, acc_ref, qb):
    stat_ref[qb, 0:1, :] = state[0]
    stat_ref[qb, 1:2, :] = state[1]
    acc_ref[qb] = state[2]


def load_state(stat_ref, acc_ref, qb):
    return stat_ref[qb, 0:1, :], stat_ref[qb, 1:2, :], acc_ref[qb]


def parts_of(x):
    high = x.astype(BF).astype(F32)
    rest = x - high
    middle = rest.astype(BF).astype(F32)
    return high, middle, (rest - middle).astype(BF).astype(F32)


def store_packed(state, ref, qb):
    best, total, product = state
    ref[qb, 0:AHDIM, :] = (product / jnp.where(total > 0.0, total, 1.0)).astype(BF)
    row = lax.broadcasted_iota(jnp.int32, (16, TOK), 0)
    stats = jnp.zeros((16, TOK), F32)
    for i, part in enumerate(parts_of(best) + parts_of(total)):
        stats = jnp.where(row == i, part, stats)
    ref[qb, AHDIM:PACK, :] = stats.astype(BF)


def merge_packed(state, ref, qb):
    stats = ref[qb, AHDIM:PACK, :].astype(F32)
    best = stats[0:1] + stats[1:2] + stats[2:3]
    total = stats[3:4] + stats[4:5] + stats[5:6]
    best = jnp.where(total > 0.0, best, LOWEST)
    top = jnp.maximum(best, state[0])
    other = jnp.exp2((best - top) * SCALE) * total
    mine = jnp.exp2((state[0] - top) * SCALE)
    product = state[2] * mine + ref[qb, 0:AHDIM, :].astype(F32) * other
    return top, state[1] * mine + other, product


def own_kernel(kv_ref, q_ref, second_ref, a_stat, a_acc, b_stat, b_acc):
    a_keys, b_keys = keys_of(kv_ref, 0), keys_of(second_ref, AHDIM)
    for qb in range(ROW):
        state = absorb(
            second_ref[qb, 0:AHDIM, :],
            a_keys,
            rows_of(kv_ref, AHDIM),
            "causal",
            qb,
            None,
        )
        store_state(state, a_stat, a_acc, qb)
        state = absorb(
            q_ref[qb],
            b_keys,
            rows_of(second_ref, 2 * AHDIM),
            "causal",
            qb,
            None,
        )
        store_state(state, b_stat, b_acc, qb)


def nearer_kernel(row_ref, second_ref, kv_ref, stat_in, acc_in, stat_ref, acc_ref):
    stat_ref[...] = stat_in[...]
    acc_ref[...] = acc_in[...]

    @pl.when(row_ref[0] >= 1)
    def _():
        keys = keys_of(kv_ref, 0)
        for qb in range(ROW):
            state = absorb(
                second_ref[qb, 0:AHDIM, :],
                keys,
                rows_of(kv_ref, AHDIM),
                "full",
                qb,
                load_state(stat_in, acc_in, qb),
            )
            store_state(state, stat_ref, acc_ref, qb)


def next_kernel(q_ref, second_ref, stat_ref, acc_ref):
    keys = keys_of(second_ref, AHDIM)
    for qb in range(ROW):
        state = absorb(
            q_ref[qb],
            keys,
            rows_of(second_ref, 2 * AHDIM),
            "full",
            qb,
            None,
        )
        store_state(state, stat_ref, acc_ref, qb)


def after_kernel(q_ref, second_ref, packed_ref):
    keys = keys_of(second_ref, AHDIM)
    for qb in range(ROW):
        state = absorb(
            q_ref[qb],
            keys,
            rows_of(second_ref, 2 * AHDIM),
            "tail",
            qb,
            None,
        )
        store_packed(state, packed_ref, qb)


def join_kernel(stat_in, acc_in, packed_in, packed_ref):
    for qb in range(ROW):
        store_packed(merge_packed(load_state(stat_in, acc_in, qb), packed_in, qb), packed_ref, qb)


def last_kernel(
    row_ref, place_ref, second_ref, kv_ref, a_stat, a_acc, b_stat, b_acc, packed_in, *refs
):
    out_ref = refs[ROW]
    for qb in range(ROW):
        _, total, product = merge_packed(load_state(b_stat, b_acc, qb), packed_in, qb)
        out_ref[qb, AHDIM : 2 * AHDIM, :] = (product / total).astype(BF)
        _, total, product = load_state(a_stat, a_acc, qb)
        out_ref[qb, 0:AHDIM, :] = (product / total).astype(BF)

    @pl.when(row_ref[0] >= 2)
    def _():
        keys = keys_of(kv_ref, 0)
        for qb in range(ROW):
            _, total, product = absorb(
                second_ref[qb, 0:AHDIM, :],
                keys,
                rows_of(kv_ref, AHDIM),
                "tail",
                qb,
                load_state(a_stat, a_acc, qb),
            )
            out_ref[qb, 0:AHDIM, :] = (product / total).astype(BF)

    for d in range(ROW):
        refs[d][...] = out_ref[lax.rem(place_ref[0] + d, ROW)]


def back_kernel(place_ref, *refs):
    out_ref, turned = refs[ROW:]
    for d in range(ROW):
        pair = lax.rem(place_ref[0] + ROW - d, ROW)
        at = pl.multiple_of(pair * (2 * AHDIM), 32)
        turned[pl.ds(at, 2 * AHDIM), :] = refs[d][...]
    for start in range(0, turned.shape[0], 128):
        out_ref[:, start : start + 128] = turned[start : start + 128, :].T


def blocks_kernel(owner_ref, k_ref, v_ref, state_ref, send_ref, later_ref, slots, later):
    owners = owner_ref.shape[1]
    pieces = k_ref.shape[1] // 128
    rows, later_rows = slots.shape[0] // owners, later.shape[0] // owners
    owner = lax.broadcasted_iota(jnp.int32, (owners, owners), 0)
    pick = (owner_ref[...] == owner).astype(BF)
    block = lax.broadcasted_iota(jnp.int32, (owners, 2 * owners), 0)
    at = lax.broadcasted_iota(jnp.int32, (owners, 2 * owners), 1)
    for i in range(2):
        places = jnp.dot(pick, (at == 2 * block + i).astype(BF), preferred_element_type=F32)
        places = places.astype(BF)
        for kind, ref in enumerate((k_ref, v_ref)):
            picked = jnp.dot(places, ref[...], preferred_element_type=F32)
            for j in range(pieces):
                tile = picked[:, j * 128 : (j + 1) * 128]
                if j < FIRST:
                    slots[pl.ds((i * FIRST + j) * 2 + kind, owners, stride=rows), :] = tile
                else:
                    row = (i * (pieces - FIRST) + j - FIRST) * 2 + kind
                    later[pl.ds(row, owners, stride=later_rows), :] = tile
    for device in range(owners):
        slots[(device + 1) * rows - 8 : (device + 1) * rows, :] = state_ref[
            device * 8 : (device + 1) * 8, :
        ]
        later[(device + 1) * later_rows - 8 : (device + 1) * later_rows, :] = jnp.zeros(
            (8, 128), F32
        )
    send_ref[...] = slots[...].astype(BF)
    later_ref[...] = later[...].astype(BF)


def expand(x, heads):
    head = lax.broadcasted_iota(jnp.int32, (heads, heads * HDIM), 0)
    column = lax.broadcasted_iota(jnp.int32, (heads, heads * HDIM), 1)
    hot = (column // HDIM == head).astype(F32)
    return jnp.dot(x, hot, precision=HIGHEST, preferred_element_type=F32)


def state_kernel(x_ref, rate_ref, write_ref, cum_ref, turned_ref, slots):
    heads = rate_ref.shape[0]
    half = heads // 2 * HDIM
    rate = rate_ref[...]
    first = lax.broadcasted_iota(jnp.int32, (TOK, TOK), 0)
    second = lax.broadcasted_iota(jnp.int32, (TOK, TOK), 1)
    cum_ref[...] = -jnp.dot(
        rate, (first <= second).astype(F32), precision=HIGHEST, preferred_element_type=F32
    )
    turned = -lax.dot_general(
        (second <= first).astype(F32),
        rate,
        (((1,), (1,)), ((), ())),
        precision=HIGHEST,
        preferred_element_type=F32,
    )
    turned_ref[...] = turned
    end = turned[TOK - 1 : TOK, :]
    scaled = (x_ref[...].astype(F32) * expand(jnp.exp(end - turned), heads)).astype(BF)
    local = jnp.dot(write_ref[...], scaled, preferred_element_type=F32)
    for side in range(2):
        for k in range(half // 128):
            start = side * half + k * 128
            slots[pl.ds(side * NSTATE * 8 + k, NSTATE, stride=8), :] = local[:, start : start + 128]
    lane = lax.broadcasted_iota(jnp.int32, (heads, 128), 1)
    head = lax.broadcasted_iota(jnp.int32, (heads, 128), 0)
    for side in range(2):
        tail = jnp.zeros((1, 128), F32)
        for i, part in enumerate(parts_of(end)):
            hot = (lane == 3 * (head - side * (heads // 2)) + i) & (head // (heads // 2) == side)
            tail = tail + jnp.dot(
                part, hot.astype(F32), precision=HIGHEST, preferred_element_type=F32
            )
        slots[pl.ds(side * NSTATE * 8 + half // 128, NSTATE, stride=8), :] = jnp.broadcast_to(
            tail, (NSTATE, 128)
        )


def scan_kernel(got_ref, out_ref, state, decay):
    blocks = state.shape[0] // 8
    rows = got_ref.shape[0] // blocks
    for b in range(blocks):
        state[b * 8 : (b + 1) * 8, :] = got_ref[(b + 1) * rows - 16 : (b + 1) * rows, :].astype(
            F32
        )[8:16]
    tail = state[pl.ds(7, blocks, stride=8), :].astype(BF)
    part = lax.broadcasted_iota(jnp.int32, (128, 128), 0)
    column = lax.broadcasted_iota(jnp.int32, (128, 128), 1)
    for k in range(7):
        hot = (part // 3 == 2 * k + column // HDIM).astype(BF)
        decay[pl.ds(k, blocks, stride=8), :] = jnp.exp(
            jnp.dot(tail, hot, preferred_element_type=F32)
        )
    decay[pl.ds(7, blocks, stride=8), :] = jnp.zeros((blocks, 128), F32)

    def step(b, carry):
        at = pl.ds(pl.multiple_of(b * 8, 8), 8)
        after = decay[at, :] * carry + state[at, :]
        state[at, :] = carry
        return after

    lax.fori_loop(0, blocks, step, jnp.zeros((8, 128), F32), unroll=8)
    out_ref[...] = state[...].astype(BF)


def cache_kernel(got_ref, later_ref, out_ref, pool_ref, slots, later):
    blocks = out_ref.shape[0]
    pieces = out_ref.shape[3] // 128
    for ref, held in ((got_ref, slots), (later_ref, later)):
        rows = held.shape[1]
        for k in range(blocks // 8):
            part = ref[k * 8 * rows : (k + 1) * 8 * rows, :].astype(F32)
            held[k * 8 : (k + 1) * 8] = part.reshape(8, rows, 128)
    for i in range(2):
        for j in range(pieces):
            held, row = (
                (slots, (i * FIRST + j) * 2)
                if j < FIRST
                else (later, (i * (pieces - FIRST) + j - FIRST) * 2)
            )
            out_ref[:, i, :, j * 128 : (j + 1) * 128] = held[:, row : row + 2, :].astype(BF)
    for k in range(7):
        pool_ref[0, :, k * 128 : (k + 1) * 128] = later[:, later.shape[1] - 8 + k, :]


def inner_kernel(
    spot_ref, x_ref, cum_ref, turned_ref, write_ref, read_ref, gain_ref, out_ref, spot_ref_out
):
    heads = cum_ref.shape[0]
    write = write_ref[...]
    turned = turned_ref[...]
    gram = lax.dot_general(
        read_ref[...], write, (((0,), (0,)), ((), ())), preferred_element_type=F32
    )
    t_at = lax.broadcasted_iota(jnp.int32, (TOK, TOK), 0)
    s_at = lax.broadcasted_iota(jnp.int32, (TOK, TOK), 1)
    later = t_at >= s_at
    left = lax.broadcasted_iota(jnp.int32, (TOK, 2 * HDIM), 1) < HDIM
    gain = expand(gain_ref[...], heads)
    for pair in range(heads // 2):
        columns = slice(pair * 2 * HDIM, (pair + 1) * 2 * HDIM)
        x = x_ref[:, columns]
        inner = []
        for h in (2 * pair, 2 * pair + 1):
            spread = jnp.where(later, turned[:, h : h + 1] - cum_ref[h : h + 1, :], LOWEST)
            weights = (gram * jnp.exp(spread)).astype(BF)
            inner.append(jnp.dot(weights, x, preferred_element_type=F32))
        out_ref[:, columns] = jnp.where(left, inner[0], inner[1]) + gain[:, columns] * x.astype(
            F32
        )
    spot = spot_ref[0]
    position = lax.broadcasted_iota(jnp.int32, (TOK, heads), 0)
    to_spot = jnp.exp(jnp.where(position <= spot, spot_log(turned, spot) - turned, LOWEST))
    scaled = (x_ref[...].astype(F32) * expand(to_spot, heads)).astype(BF)
    spot_ref_out[...] = jnp.dot(write, scaled, preferred_element_type=F32)


def spot_log(turned, spot):
    position = lax.broadcasted_iota(jnp.int32, turned.shape, 0)
    return jnp.sum(jnp.where(position == spot, turned, 0.0), axis=0, keepdims=True)


def arrived(came_ref, slots, heads):
    half = heads // 2 * HDIM
    slots[...] = came_ref[...].astype(F32)
    return jnp.concatenate(
        [
            slots[pl.ds(side * NSTATE * 8 + k, NSTATE, stride=8), :]
            for side in range(2)
            for k in range(half // 128)
        ],
        axis=1,
    )


def mixer_kernel(turned_ref, read_ref, inner_ref, came_ref, out_ref, slots):
    heads = turned_ref.shape[1]
    arriving = arrived(came_ref, slots, heads).astype(BF)
    carried = lax.dot_general(
        read_ref[...], arriving, (((0,), (0,)), ((), ())), preferred_element_type=F32
    )
    out_ref[...] = inner_ref[...] + carried * expand(jnp.exp(turned_ref[...]), heads)


def spot_kernel(
    spot_ref, owner_ref, turned_ref, local_ref, came_ref, later_ref, send_ref, slots, rows, flat, later
):
    heads = turned_ref.shape[1]
    arriving = arrived(came_ref, slots, heads)
    at_spot = expand(jnp.exp(spot_log(turned_ref[...], spot_ref[0])), heads)
    state = arriving * at_spot + local_ref[...]
    rows[:, 0:NSTATE] = state.T
    even = rows[pl.ds(0, heads * HDIM // 2, stride=2), :]
    odd = pltpu.roll(rows[pl.ds(1, heads * HDIM // 2, stride=2), :], NSTATE, 1)
    lane = lax.broadcasted_iota(jnp.int32, even.shape, 1)
    flat[0 : heads * HDIM // 2, :] = jnp.where(lane < NSTATE, even, odd)
    later[...] = later_ref[...].astype(F32)
    owners = owner_ref.shape[1]
    each = later.shape[0] // owners
    for piece in range(owners):
        at = pl.multiple_of(owner_ref[0, piece] * each + each - 8, 8)
        later[pl.ds(at, 8), :] = flat[7 * piece : 7 * piece + 8, :]
    send_ref[...] = later[...].astype(BF)


def to_all(x):
    return lax.all_to_all(x, "seq", split_axis=0, concat_axis=0, tiled=True)


def in_row(parts):
    count = lax.axis_size("seq")
    return [parts[0]] + [
        lax.ppermute(
            parts[d],
            "seq",
            [(i, i // ROW * ROW + (i + d) % ROW) for i in range(count)],
        )
        for d in range(1, ROW)
    ]


def shift(x, distance):
    devices = range(lax.axis_size("seq"))
    return lax.ppermute(x, "seq", [(i - distance, i) for i in devices if i - distance in devices])


def body(
    mixer_input,
    decay_rate,
    state_in,
    state_out,
    skip_gain,
    att_queries,
    att_keys,
    att_values,
    checkpoint_at,
    checkpoint_owner,
    block_owner,
):
    position = lax.axis_index("seq")
    owners = lax.axis_size("seq")
    tokens, width = mixer_input.shape
    heads = decay_rate.shape[0]
    row = (position // ROW).astype(jnp.int32)[None]

    place = (position % ROW).astype(jnp.int32)[None]
    parts, _ = call(
        prep_kernel,
        (shape(6 * AHDIM, TOK),) * ROW,
        (0,),
        place,
        att_queries,
        att_keys,
        att_values,
        name="prep",
        scratch=[pltpu.VMEM((width, TOK), BF)] * 3,
    )
    parts = in_row(parts)

    block_len = tokens // owners
    lanes = width // 128
    rows, later_rows = 4 * FIRST + 8, 4 * (lanes - FIRST) + 8
    (cum, turned, state_send), _ = call(
        state_kernel,
        (
            shape(heads, TOK, dtype=F32),
            shape(TOK, heads, dtype=F32),
            shape(owners * 8, 128, dtype=F32),
        ),
        (),
        mixer_input,
        decay_rate,
        state_in.T,
        name="state",
    )
    (send, later), sent = call(
        blocks_kernel,
        (shape(owners * rows, 128), shape(owners * later_rows, 128)),
        (),
        block_owner,
        att_keys,
        att_values,
        state_send,
        name="blocks",
        scratch=[
            pltpu.VMEM((owners * rows, 128), F32),
            pltpu.VMEM((owners * later_rows, 128), F32),
        ],
        mib=24,
    )
    spot = (checkpoint_at - position * tokens).astype(jnp.int32)
    (inner, spot_local), inner_done = call(
        inner_kernel,
        (shape(tokens, width, dtype=F32), shape(NSTATE, width, dtype=F32)),
        (0,),
        spot,
        mixer_input,
        cum,
        turned,
        state_in.T,
        state_out.T,
        skip_gain[None, :],
        name="inner",
        after=(sent,),
    )
    got = to_all(send.reshape(owners, rows, 128)).reshape(-1, 128)

    (kv_own, q_own, second), _ = call(
        gather_kernel,
        (shape(ROW, 2 * AHDIM, TOK), shape(ROW, AHDIM, TOK), shape(ROW, 3 * AHDIM, TOK)),
        (0,),
        place,
        *parts,
        name="gather",
        after=(inner_done,),
    )
    kv_near = shift(kv_own, ROW)
    q_next = shift(q_own, -ROW)
    kv_far = shift(kv_near, ROW)
    q_after = shift(q_next, -ROW)
    stat, acc = shape(ROW, 8, TOK, dtype=F32), shape(ROW, AHDIM, TOK, dtype=F32)
    packed = shape(ROW, PACK, TOK)
    (a_stat, a_acc, b_stat, b_acc), own_done = call(
        own_kernel, (stat, acc, stat, acc), (), kv_own, q_own, second, name="own", flops=HEAVY
    )
    (n_stat, n_acc), next_done = call(
        next_kernel, (stat, acc), (), q_next, second, name="next", flops=HEAVY, after=(own_done,)
    )
    entering, scanned = call(
        scan_kernel,
        shape(owners * 8, 128),
        (),
        got,
        name="scan",
        scratch=[pltpu.VMEM((owners * 8, 128), F32)] * 2,
        after=(next_done,),
    )
    came = to_all(entering.reshape(owners, 8, 128)).reshape(owners * 8, 128)
    after, _ = call(after_kernel, packed, (), q_after, second, name="after", after=(scanned,))
    after = shift(after, ROW)
    (a_stat, a_acc), near_done = call(
        nearer_kernel, (stat, acc), (0,), row, second, kv_near, a_stat, a_acc, name="nearer"
    )
    mixer_out, mixer_done = call(
        mixer_kernel,
        shape(tokens, width, dtype=F32),
        (),
        turned,
        state_out.T,
        inner,
        came,
        name="mixer",
        scratch=[pltpu.VMEM((owners * 8, 128), F32)],
    )
    join_send, joined_done = call(
        join_kernel,
        packed,
        (),
        n_stat,
        n_acc,
        after,
        name="join",
        flops=HEAVY,
        after=(mixer_done, near_done),
    )
    joined = shift(join_send, ROW)

    pool_send, _ = call(
        spot_kernel,
        shape(owners * later_rows, 128),
        (0, 1),
        spot,
        checkpoint_owner,
        turned,
        spot_local,
        came,
        later,
        name="spot",
        scratch=[
            pltpu.VMEM((owners * 8, 128), F32),
            pltpu.VMEM((width, 2 * NSTATE), F32),
            pltpu.VMEM((width // 2 + 8, 128), F32),
            pltpu.VMEM((owners * later_rows, 128), F32),
        ],
        after=(joined_done,),
    )
    later_got = to_all(pool_send.reshape(owners, later_rows, 128)).reshape(-1, 128)

    out, _ = call(
        last_kernel,
        (shape(2 * AHDIM, TOK),) * ROW,
        (0, 1),
        row,
        place,
        second,
        kv_far,
        a_stat,
        a_acc,
        b_stat,
        b_acc,
        joined,
        name="last",
        flops=HEAVY,
        scratch=[pltpu.VMEM((ROW, 2 * AHDIM, TOK), BF)],
    )
    attention_out, _ = call(
        back_kernel,
        shape(TOK, width),
        (0,),
        place,
        *in_row(out),
        name="back",
        scratch=[pltpu.VMEM((width, TOK), BF)],
    )
    (cache_pool, state_pool), _ = call(
        cache_kernel,
        (shape(owners, block_len, 2, width), shape(1, owners, width // 2, dtype=F32)),
        (),
        got,
        later_got,
        name="cache",
        scratch=[
            pltpu.VMEM((owners, rows, 128), F32),
            pltpu.VMEM((owners, later_rows, 128), F32),
        ],
        mib=24,
    )
    cache_pool = cache_pool.reshape(1, owners * block_len, 2, width)
    return (mixer_out, attention_out, state_pool, cache_pool)


def solution(mesh):
    placed = (
        P("seq", "head"),
        P("head", "seq"),
        P("seq", "head"),
        P("seq", "head"),
        P("head"),
        P("seq", "head"),
        P("seq", "head"),
        P("seq", "head"),
        P("seq"),
        P("seq", None),
        P("seq", None),
    )
    return jax.shard_map(
        body,
        mesh=mesh,
        in_specs=placed,
        out_specs=(
            P("seq", "head"),
            P("seq", "head"),
            P("seq", None, "head"),
            P("seq", None, None, "head"),
        ),
        check_vma=False,
    )
```

```python
import functools

import jax
import jax.numpy as jnp
from jax import lax
from jax.experimental import pallas as pl
from jax.experimental.pallas import tpu as pltpu
from jax.sharding import PartitionSpec as P

HDIM = 64
NSTATE = 64
AHDIM = 224
TOK = 256
ROW = 4
PACK = AHDIM + 16
SCALE = AHDIM**-0.5 * 1.4426950408889634
LOWEST = -1e30
HEAVY = 4 * 10**10
FIRST = 6
BF = jnp.bfloat16
F32 = jnp.float32
HIGHEST = lax.Precision.HIGHEST


def call(kernel, out_shape, in_smem, *args, name, scratch=(), after=(), mib=16, flops=0):
    specs = [
        pl.BlockSpec(memory_space=pltpu.SMEM if i in in_smem else pltpu.VMEM)
        for i in range(len(args))
    ] + [pl.BlockSpec(memory_space=pl.ANY)] * len(after)

    many = isinstance(out_shape, tuple)
    out_shapes = (out_shape if many else (out_shape,)) + (shape(8, 128, dtype=F32),)
    first_out = len(args) + len(after)
    token = first_out + len(out_shapes) - 1

    def run(*refs):
        kernel(*refs[: len(args)], *refs[first_out:token], *refs[token + 1 :])
        refs[token][...] = jnp.zeros((8, 128), F32)

    results = pl.pallas_call(
        run,
        out_shape=out_shapes,
        in_specs=specs,
        out_specs=tuple(pl.BlockSpec(memory_space=pltpu.VMEM) for _ in out_shapes),
        scratch_shapes=list(scratch),
        compiler_params=pltpu.CompilerParams(vmem_limit_bytes=mib * 2**20),
        cost_estimate=pl.CostEstimate(flops=flops, bytes_accessed=0, transcendentals=0),
        name=name,
    )(*args, *after)
    return (results[:-1] if many else results[0]), results[-1]


def shape(*dims, dtype=BF):
    return jax.ShapeDtypeStruct(dims, dtype)


def turn(x_ref, turned):
    for start in range(0, x_ref.shape[1], 128):
        turned[start : start + 128, :] = x_ref[:, start : start + 128].T


def pair_rows(turned, pair, odd):
    at = pair * (2 * AHDIM) + odd * AHDIM
    return turned[pl.ds(pl.multiple_of(at, 32), AHDIM), :]


def prep_kernel(place_ref, q_ref, k_ref, v_ref, *refs):
    outputs, (q, k, v) = refs[:ROW], refs[ROW:]
    for x_ref, turned in ((k_ref, k), (v_ref, v), (q_ref, q)):
        turn(x_ref, turned)
    for d in range(ROW):
        pair = lax.rem(place_ref[0] + d, ROW)
        for i, (turned, odd) in enumerate(((k, 0), (v, 0), (q, 1), (q, 0), (k, 1), (v, 1))):
            outputs[d][i * AHDIM : (i + 1) * AHDIM, :] = pair_rows(turned, pair, odd)


def gather_kernel(place_ref, *refs):
    kv_ref, q_ref, second_ref = refs[ROW:]
    for d in range(ROW):
        block = lax.rem(place_ref[0] + ROW - d, ROW)
        kv_ref[block] = refs[d][0 : 2 * AHDIM, :]
        q_ref[block] = refs[d][2 * AHDIM : 3 * AHDIM, :]
        second_ref[block] = refs[d][3 * AHDIM : 6 * AHDIM, :]


def absorb(q, keys, values, mode, qb, state):
    if mode == "causal":
        blocks = range(0, qb + 1)
    elif mode == "tail":
        blocks = range(qb, ROW)
    else:
        blocks = range(ROW)
    scores = []
    for kb in blocks:
        s = jnp.dot(keys(kb), q, preferred_element_type=F32)
        if kb == qb and mode != "full":
            s_at = lax.broadcasted_iota(jnp.int32, s.shape, 0)
            t_at = lax.broadcasted_iota(jnp.int32, s.shape, 1)
            s = jnp.where(s_at <= t_at if mode == "causal" else s_at > t_at, s, LOWEST)
        scores.append(s)
    best = functools.reduce(jnp.maximum, [jnp.max(s, axis=0, keepdims=True) for s in scores])
    if state is not None:
        best = jnp.maximum(best, state[0])
    total, product = 0.0, 0.0
    for kb, s in zip(blocks, scores):
        p = jnp.exp2((s - best) * SCALE)
        if kb == qb and mode == "tail":
            s_at = lax.broadcasted_iota(jnp.int32, s.shape, 0)
            t_at = lax.broadcasted_iota(jnp.int32, s.shape, 1)
            p = jnp.where(s_at > t_at, p, 0.0)
        total = total + jnp.sum(p, axis=0, keepdims=True)
        product = product + jnp.dot(values(kb), p.astype(BF), preferred_element_type=F32)
    if state is not None:
        shrink = jnp.exp2((state[0] - best) * SCALE)
        total = total + state[1] * shrink
        product = product + state[2] * shrink
    return best, total, product


def rows_of(ref, first):
    return lambda kb: ref[kb, first : first + AHDIM, :]


def keys_of(ref, first):
    turned = [ref[kb, first : first + AHDIM, :].T for kb in range(ROW)]
    return lambda kb: turned[kb]


def store_state(state, stat_ref, acc_ref, qb):
    stat_ref[qb, 0:1, :] = state[0]
    stat_ref[qb, 1:2, :] = state[1]
    acc_ref[qb] = state[2]


def load_state(stat_ref, acc_ref, qb):
    return stat_ref[qb, 0:1, :], stat_ref[qb, 1:2, :], acc_ref[qb]


def parts_of(x):
    high = x.astype(BF).astype(F32)
    rest = x - high
    middle = rest.astype(BF).astype(F32)
    return high, middle, (rest - middle).astype(BF).astype(F32)


def store_packed(state, ref, qb):
    best, total, product = state
    ref[qb, 0:AHDIM, :] = (product / jnp.where(total > 0.0, total, 1.0)).astype(BF)
    row = lax.broadcasted_iota(jnp.int32, (16, TOK), 0)
    stats = jnp.zeros((16, TOK), F32)
    for i, part in enumerate(parts_of(best) + parts_of(total)):
        stats = jnp.where(row == i, part, stats)
    ref[qb, AHDIM:PACK, :] = stats.astype(BF)


def merge_packed(state, ref, qb):
    stats = ref[qb, AHDIM:PACK, :].astype(F32)
    best = stats[0:1] + stats[1:2] + stats[2:3]
    total = stats[3:4] + stats[4:5] + stats[5:6]
    best = jnp.where(total > 0.0, best, LOWEST)
    top = jnp.maximum(best, state[0])
    other = jnp.exp2((best - top) * SCALE) * total
    mine = jnp.exp2((state[0] - top) * SCALE)
    product = state[2] * mine + ref[qb, 0:AHDIM, :].astype(F32) * other
    return top, state[1] * mine + other, product


def own_kernel(kv_ref, q_ref, second_ref, a_stat, a_acc, b_stat, b_acc):
    a_keys, b_keys = keys_of(kv_ref, 0), keys_of(second_ref, AHDIM)
    for qb in range(ROW):
        state = absorb(
            second_ref[qb, 0:AHDIM, :],
            a_keys,
            rows_of(kv_ref, AHDIM),
            "causal",
            qb,
            None,
        )
        store_state(state, a_stat, a_acc, qb)
        state = absorb(
            q_ref[qb],
            b_keys,
            rows_of(second_ref, 2 * AHDIM),
            "causal",
            qb,
            None,
        )
        store_state(state, b_stat, b_acc, qb)


def nearer_kernel(row_ref, second_ref, kv_ref, stat_in, acc_in, stat_ref, acc_ref):
    stat_ref[...] = stat_in[...]
    acc_ref[...] = acc_in[...]

    @pl.when(row_ref[0] >= 1)
    def _():
        keys = keys_of(kv_ref, 0)
        for qb in range(ROW):
            state = absorb(
                second_ref[qb, 0:AHDIM, :],
                keys,
                rows_of(kv_ref, AHDIM),
                "full",
                qb,
                load_state(stat_in, acc_in, qb),
            )
            store_state(state, stat_ref, acc_ref, qb)


def next_kernel(q_ref, second_ref, stat_ref, acc_ref):
    keys = keys_of(second_ref, AHDIM)
    for qb in range(ROW):
        state = absorb(
            q_ref[qb],
            keys,
            rows_of(second_ref, 2 * AHDIM),
            "full",
            qb,
            None,
        )
        store_state(state, stat_ref, acc_ref, qb)


def after_kernel(q_ref, second_ref, packed_ref):
    keys = keys_of(second_ref, AHDIM)
    for qb in range(ROW):
        state = absorb(
            q_ref[qb],
            keys,
            rows_of(second_ref, 2 * AHDIM),
            "tail",
            qb,
            None,
        )
        store_packed(state, packed_ref, qb)


def join_kernel(stat_in, acc_in, packed_in, packed_ref):
    for qb in range(ROW):
        store_packed(merge_packed(load_state(stat_in, acc_in, qb), packed_in, qb), packed_ref, qb)


def give(place_ref, refs, held):
    for d in range(ROW):
        refs[d][...] = held[lax.rem(place_ref[0] + d, ROW)]


def last_even_kernel(row_ref, place_ref, second_ref, kv_ref, stat_ref, acc_ref, *refs):
    held = refs[ROW]
    for qb in range(ROW):
        _, total, product = load_state(stat_ref, acc_ref, qb)
        held[qb] = (product / total).astype(BF)

    @pl.when(row_ref[0] >= 2)
    def _():
        keys = keys_of(kv_ref, 0)
        for qb in range(ROW):
            _, total, product = absorb(
                second_ref[qb, 0:AHDIM, :],
                keys,
                rows_of(kv_ref, AHDIM),
                "tail",
                qb,
                load_state(stat_ref, acc_ref, qb),
            )
            held[qb] = (product / total).astype(BF)

    give(place_ref, refs, held)


def last_odd_kernel(place_ref, stat_ref, acc_ref, packed_ref, *refs):
    held = refs[ROW]
    for qb in range(ROW):
        _, total, product = merge_packed(load_state(stat_ref, acc_ref, qb), packed_ref, qb)
        held[qb] = (product / total).astype(BF)
    give(place_ref, refs, held)


def back_kernel(place_ref, *refs):
    out_ref, turned = refs[2 * ROW :]
    for d in range(ROW):
        pair = lax.rem(place_ref[0] + ROW - d, ROW)
        for odd in range(2):
            at = pl.multiple_of(pair * (2 * AHDIM) + odd * AHDIM, 32)
            turned[pl.ds(at, AHDIM), :] = refs[odd * ROW + d][...]
    for start in range(0, turned.shape[0], 128):
        out_ref[:, start : start + 128] = turned[start : start + 128, :].T


def blocks_kernel(owner_ref, k_ref, v_ref, state_ref, send_ref, later_ref, slots, later):
    owners = owner_ref.shape[1]
    pieces = k_ref.shape[1] // 128
    rows, later_rows = slots.shape[0] // owners, later.shape[0] // owners
    owner = lax.broadcasted_iota(jnp.int32, (owners, owners), 0)
    pick = (owner_ref[...] == owner).astype(BF)
    block = lax.broadcasted_iota(jnp.int32, (owners, 2 * owners), 0)
    at = lax.broadcasted_iota(jnp.int32, (owners, 2 * owners), 1)
    for i in range(2):
        places = jnp.dot(pick, (at == 2 * block + i).astype(BF), preferred_element_type=F32)
        places = places.astype(BF)
        for kind, ref in enumerate((k_ref, v_ref)):
            picked = jnp.dot(places, ref[...], preferred_element_type=F32)
            for j in range(pieces):
                tile = picked[:, j * 128 : (j + 1) * 128]
                if j < FIRST:
                    slots[pl.ds((i * FIRST + j) * 2 + kind, owners, stride=rows), :] = tile
                else:
                    row = (i * (pieces - FIRST) + j - FIRST) * 2 + kind
                    later[pl.ds(row, owners, stride=later_rows), :] = tile
    for device in range(owners):
        slots[(device + 1) * rows - 8 : (device + 1) * rows, :] = state_ref[
            device * 8 : (device + 1) * 8, :
        ]
        later[(device + 1) * later_rows - 8 : (device + 1) * later_rows, :] = jnp.zeros(
            (8, 128), F32
        )
    send_ref[...] = slots[...].astype(BF)
    later_ref[...] = later[...].astype(BF)


def expand(x, heads):
    head = lax.broadcasted_iota(jnp.int32, (heads, heads * HDIM), 0)
    column = lax.broadcasted_iota(jnp.int32, (heads, heads * HDIM), 1)
    hot = (column // HDIM == head).astype(F32)
    return jnp.dot(x, hot, precision=HIGHEST, preferred_element_type=F32)


def state_kernel(x_ref, rate_ref, write_ref, cum_ref, turned_ref, slots):
    heads = rate_ref.shape[0]
    half = heads // 2 * HDIM
    rate = rate_ref[...]
    first = lax.broadcasted_iota(jnp.int32, (TOK, TOK), 0)
    second = lax.broadcasted_iota(jnp.int32, (TOK, TOK), 1)
    cum_ref[...] = -jnp.dot(
        rate, (first <= second).astype(F32), precision=HIGHEST, preferred_element_type=F32
    )
    turned = -lax.dot_general(
        (second <= first).astype(F32),
        rate,
        (((1,), (1,)), ((), ())),
        precision=HIGHEST,
        preferred_element_type=F32,
    )
    turned_ref[...] = turned
    end = turned[TOK - 1 : TOK, :]
    scaled = (x_ref[...].astype(F32) * expand(jnp.exp(end - turned), heads)).astype(BF)
    local = jnp.dot(write_ref[...], scaled, preferred_element_type=F32)
    for side in range(2):
        for k in range(half // 128):
            start = side * half + k * 128
            slots[pl.ds(side * NSTATE * 8 + k, NSTATE, stride=8), :] = local[:, start : start + 128]
    lane = lax.broadcasted_iota(jnp.int32, (heads, 128), 1)
    head = lax.broadcasted_iota(jnp.int32, (heads, 128), 0)
    for side in range(2):
        tail = jnp.zeros((1, 128), F32)
        for i, part in enumerate(parts_of(end)):
            hot = (lane == 3 * (head - side * (heads // 2)) + i) & (head // (heads // 2) == side)
            tail = tail + jnp.dot(
                part, hot.astype(F32), precision=HIGHEST, preferred_element_type=F32
            )
        slots[pl.ds(side * NSTATE * 8 + half // 128, NSTATE, stride=8), :] = jnp.broadcast_to(
            tail, (NSTATE, 128)
        )


def scan_kernel(got_ref, out_ref, state, decay):
    blocks = state.shape[0] // 8
    rows = got_ref.shape[0] // blocks
    for b in range(blocks):
        state[b * 8 : (b + 1) * 8, :] = got_ref[(b + 1) * rows - 16 : (b + 1) * rows, :].astype(
            F32
        )[8:16]
    tail = state[pl.ds(7, blocks, stride=8), :].astype(BF)
    part = lax.broadcasted_iota(jnp.int32, (128, 128), 0)
    column = lax.broadcasted_iota(jnp.int32, (128, 128), 1)
    for k in range(7):
        hot = (part // 3 == 2 * k + column // HDIM).astype(BF)
        decay[pl.ds(k, blocks, stride=8), :] = jnp.exp(
            jnp.dot(tail, hot, preferred_element_type=F32)
        )
    decay[pl.ds(7, blocks, stride=8), :] = jnp.zeros((blocks, 128), F32)

    def step(b, carry):
        at = pl.ds(pl.multiple_of(b * 8, 8), 8)
        after = decay[at, :] * carry + state[at, :]
        state[at, :] = carry
        return after

    lax.fori_loop(0, blocks, step, jnp.zeros((8, 128), F32), unroll=8)
    out_ref[...] = state[...].astype(BF)


def spread(ref, held, out_ref, start, count):
    blocks, rows = held.shape[0], held.shape[1]
    for k in range(blocks // 8):
        part = ref[k * 8 * rows : (k + 1) * 8 * rows, :].astype(F32)
        held[k * 8 : (k + 1) * 8] = part.reshape(8, rows, 128)
    for i in range(2):
        for j in range(count):
            row = (i * count + j) * 2
            at = (start + j) * 128
            out_ref[:, i, :, at : at + 128] = held[:, row : row + 2, :].astype(BF)


def columns_kernel(got_ref, out_ref, slots):
    spread(got_ref, slots, out_ref, 0, FIRST)


def cache_kernel(columns_ref, later_ref, out_ref, pool_ref, later):
    out_ref[:, :, :, 0 : FIRST * 128] = columns_ref[...]
    spread(later_ref, later, out_ref, FIRST, out_ref.shape[3] // 128 - FIRST)
    for k in range(7):
        pool_ref[0, :, k * 128 : (k + 1) * 128] = later[:, later.shape[1] - 8 + k, :]


def inner_kernel(
    spot_ref, x_ref, cum_ref, turned_ref, write_ref, read_ref, gain_ref, out_ref, spot_ref_out
):
    heads = cum_ref.shape[0]
    write = write_ref[...]
    turned = turned_ref[...]
    gram = lax.dot_general(
        read_ref[...], write, (((0,), (0,)), ((), ())), preferred_element_type=F32
    )
    t_at = lax.broadcasted_iota(jnp.int32, (TOK, TOK), 0)
    s_at = lax.broadcasted_iota(jnp.int32, (TOK, TOK), 1)
    later = t_at >= s_at
    left = lax.broadcasted_iota(jnp.int32, (TOK, 2 * HDIM), 1) < HDIM
    gain = expand(gain_ref[...], heads)
    for pair in range(heads // 2):
        columns = slice(pair * 2 * HDIM, (pair + 1) * 2 * HDIM)
        x = x_ref[:, columns]
        inner = []
        for h in (2 * pair, 2 * pair + 1):
            spread = jnp.where(later, turned[:, h : h + 1] - cum_ref[h : h + 1, :], LOWEST)
            weights = (gram * jnp.exp(spread)).astype(BF)
            inner.append(jnp.dot(weights, x, preferred_element_type=F32))
        out_ref[:, columns] = jnp.where(left, inner[0], inner[1]) + gain[:, columns] * x.astype(
            F32
        )
    spot = spot_ref[0]
    position = lax.broadcasted_iota(jnp.int32, (TOK, heads), 0)
    to_spot = jnp.exp(jnp.where(position <= spot, spot_log(turned, spot) - turned, LOWEST))
    scaled = (x_ref[...].astype(F32) * expand(to_spot, heads)).astype(BF)
    spot_ref_out[...] = jnp.dot(write, scaled, preferred_element_type=F32)


def spot_log(turned, spot):
    position = lax.broadcasted_iota(jnp.int32, turned.shape, 0)
    return jnp.sum(jnp.where(position == spot, turned, 0.0), axis=0, keepdims=True)


def arrived(came_ref, slots, heads):
    half = heads // 2 * HDIM
    slots[...] = came_ref[...].astype(F32)
    return jnp.concatenate(
        [
            slots[pl.ds(side * NSTATE * 8 + k, NSTATE, stride=8), :]
            for side in range(2)
            for k in range(half // 128)
        ],
        axis=1,
    )


def mixer_kernel(turned_ref, read_ref, inner_ref, came_ref, out_ref, slots):
    heads = turned_ref.shape[1]
    arriving = arrived(came_ref, slots, heads).astype(BF)
    carried = lax.dot_general(
        read_ref[...], arriving, (((0,), (0,)), ((), ())), preferred_element_type=F32
    )
    out_ref[...] = inner_ref[...] + carried * expand(jnp.exp(turned_ref[...]), heads)


def spot_kernel(
    spot_ref, owner_ref, turned_ref, local_ref, came_ref, later_ref, send_ref, slots, rows, flat, later
):
    heads = turned_ref.shape[1]
    arriving = arrived(came_ref, slots, heads)
    at_spot = expand(jnp.exp(spot_log(turned_ref[...], spot_ref[0])), heads)
    state = arriving * at_spot + local_ref[...]
    rows[:, 0:NSTATE] = state.T
    even = rows[pl.ds(0, heads * HDIM // 2, stride=2), :]
    odd = pltpu.roll(rows[pl.ds(1, heads * HDIM // 2, stride=2), :], NSTATE, 1)
    lane = lax.broadcasted_iota(jnp.int32, even.shape, 1)
    flat[0 : heads * HDIM // 2, :] = jnp.where(lane < NSTATE, even, odd)
    later[...] = later_ref[...].astype(F32)
    owners = owner_ref.shape[1]
    each = later.shape[0] // owners
    for piece in range(owners):
        at = pl.multiple_of(owner_ref[0, piece] * each + each - 8, 8)
        later[pl.ds(at, 8), :] = flat[7 * piece : 7 * piece + 8, :]
    send_ref[...] = later[...].astype(BF)


def to_all(x):
    return lax.all_to_all(x, "seq", split_axis=0, concat_axis=0, tiled=True)


def in_row(parts):
    count = lax.axis_size("seq")
    return [parts[0]] + [
        lax.ppermute(
            parts[d],
            "seq",
            [(i, i // ROW * ROW + (i + d) % ROW) for i in range(count)],
        )
        for d in range(1, ROW)
    ]


def shift(x, distance):
    devices = range(lax.axis_size("seq"))
    return lax.ppermute(x, "seq", [(i - distance, i) for i in devices if i - distance in devices])


def body(
    mixer_input,
    decay_rate,
    state_in,
    state_out,
    skip_gain,
    att_queries,
    att_keys,
    att_values,
    checkpoint_at,
    checkpoint_owner,
    block_owner,
):
    position = lax.axis_index("seq")
    owners = lax.axis_size("seq")
    tokens, width = mixer_input.shape
    heads = decay_rate.shape[0]
    row = (position // ROW).astype(jnp.int32)[None]

    place = (position % ROW).astype(jnp.int32)[None]
    parts, _ = call(
        prep_kernel,
        (shape(6 * AHDIM, TOK),) * ROW,
        (0,),
        place,
        att_queries,
        att_keys,
        att_values,
        name="prep",
        scratch=[pltpu.VMEM((width, TOK), BF)] * 3,
    )
    parts = in_row(parts)

    block_len = tokens // owners
    lanes = width // 128
    rows, later_rows = 4 * FIRST + 8, 4 * (lanes - FIRST) + 8
    (cum, turned, state_send), _ = call(
        state_kernel,
        (
            shape(heads, TOK, dtype=F32),
            shape(TOK, heads, dtype=F32),
            shape(owners * 8, 128, dtype=F32),
        ),
        (),
        mixer_input,
        decay_rate,
        state_in.T,
        name="state",
    )
    (send, later), sent = call(
        blocks_kernel,
        (shape(owners * rows, 128), shape(owners * later_rows, 128)),
        (),
        block_owner,
        att_keys,
        att_values,
        state_send,
        name="blocks",
        scratch=[
            pltpu.VMEM((owners * rows, 128), F32),
            pltpu.VMEM((owners * later_rows, 128), F32),
        ],
        mib=24,
    )
    spot = (checkpoint_at - position * tokens).astype(jnp.int32)
    (inner, spot_local), inner_done = call(
        inner_kernel,
        (shape(tokens, width, dtype=F32), shape(NSTATE, width, dtype=F32)),
        (0,),
        spot,
        mixer_input,
        cum,
        turned,
        state_in.T,
        state_out.T,
        skip_gain[None, :],
        name="inner",
        after=(sent,),
    )
    got = to_all(send.reshape(owners, rows, 128)).reshape(-1, 128)

    (kv_own, q_own, second), _ = call(
        gather_kernel,
        (shape(ROW, 2 * AHDIM, TOK), shape(ROW, AHDIM, TOK), shape(ROW, 3 * AHDIM, TOK)),
        (0,),
        place,
        *parts,
        name="gather",
        after=(inner_done,),
    )
    kv_near = shift(kv_own, ROW)
    q_next = shift(q_own, -ROW)
    kv_far = shift(kv_near, ROW)
    q_after = shift(q_next, -ROW)
    stat, acc = shape(ROW, 8, TOK, dtype=F32), shape(ROW, AHDIM, TOK, dtype=F32)
    packed = shape(ROW, PACK, TOK)
    (a_stat, a_acc, b_stat, b_acc), own_done = call(
        own_kernel, (stat, acc, stat, acc), (), kv_own, q_own, second, name="own", flops=HEAVY
    )
    (n_stat, n_acc), next_done = call(
        next_kernel, (stat, acc), (), q_next, second, name="next", flops=HEAVY, after=(own_done,)
    )
    entering, scanned = call(
        scan_kernel,
        shape(owners * 8, 128),
        (),
        got,
        name="scan",
        scratch=[pltpu.VMEM((owners * 8, 128), F32)] * 2,
        after=(next_done,),
    )
    came = to_all(entering.reshape(owners, 8, 128)).reshape(owners * 8, 128)
    after, _ = call(after_kernel, packed, (), q_after, second, name="after", after=(scanned,))
    after = shift(after, ROW)
    (a_stat, a_acc), near_done = call(
        nearer_kernel, (stat, acc), (0,), row, second, kv_near, a_stat, a_acc, name="nearer"
    )
    mixer_out, mixer_done = call(
        mixer_kernel,
        shape(tokens, width, dtype=F32),
        (),
        turned,
        state_out.T,
        inner,
        came,
        name="mixer",
        scratch=[pltpu.VMEM((owners * 8, 128), F32)],
    )
    join_send, joined_done = call(
        join_kernel,
        packed,
        (),
        n_stat,
        n_acc,
        after,
        name="join",
        flops=HEAVY,
        after=(mixer_done, near_done),
    )
    joined = shift(join_send, ROW)

    pool_send, spot_done = call(
        spot_kernel,
        shape(owners * later_rows, 128),
        (0, 1),
        spot,
        checkpoint_owner,
        turned,
        spot_local,
        came,
        later,
        name="spot",
        scratch=[
            pltpu.VMEM((owners * 8, 128), F32),
            pltpu.VMEM((width, 2 * NSTATE), F32),
            pltpu.VMEM((width // 2 + 8, 128), F32),
            pltpu.VMEM((owners * later_rows, 128), F32),
        ],
        after=(joined_done,),
    )
    later_got = to_all(pool_send.reshape(owners, later_rows, 128)).reshape(-1, 128)

    even, even_done = call(
        last_even_kernel,
        (shape(AHDIM, TOK),) * ROW,
        (0, 1),
        row,
        place,
        second,
        kv_far,
        a_stat,
        a_acc,
        name="last_even",
        scratch=[pltpu.VMEM((ROW, AHDIM, TOK), BF)],
        after=(spot_done,),
    )
    columns, columns_done = call(
        columns_kernel,
        shape(owners, block_len, 2, FIRST * 128),
        (),
        got,
        name="columns",
        scratch=[pltpu.VMEM((owners, rows, 128), F32)],
        after=(even_done,),
    )
    odd, _ = call(
        last_odd_kernel,
        (shape(AHDIM, TOK),) * ROW,
        (0,),
        place,
        b_stat,
        b_acc,
        joined,
        name="last_odd",
        flops=HEAVY,
        scratch=[pltpu.VMEM((ROW, AHDIM, TOK), BF)],
        after=(columns_done,),
    )
    attention_out, _ = call(
        back_kernel,
        shape(TOK, width),
        (0,),
        place,
        *in_row(even),
        *in_row(odd),
        name="back",
        scratch=[pltpu.VMEM((width, TOK), BF)],
    )
    (cache_pool, state_pool), _ = call(
        cache_kernel,
        (shape(owners, block_len, 2, width), shape(1, owners, width // 2, dtype=F32)),
        (),
        columns,
        later_got,
        name="cache",
        scratch=[pltpu.VMEM((owners, later_rows, 128), F32)],
        mib=24,
    )
    cache_pool = cache_pool.reshape(1, owners * block_len, 2, width)
    return (mixer_out, attention_out, state_pool, cache_pool)


def solution(mesh):
    placed = (
        P("seq", "head"),
        P("head", "seq"),
        P("seq", "head"),
        P("seq", "head"),
        P("head"),
        P("seq", "head"),
        P("seq", "head"),
        P("seq", "head"),
        P("seq"),
        P("seq", None),
        P("seq", None),
    )
    return jax.shard_map(
        body,
        mesh=mesh,
        in_specs=placed,
        out_specs=(
            P("seq", "head"),
            P("seq", "head"),
            P("seq", None, "head"),
            P("seq", None, None, "head"),
        ),
        check_vma=False,
    )
```
